512 devices in a mesh: layer: 4 (over x), row: 4 (over y_lo), col: 32 (over z, y_hi, core).
Axes of the slice: x: 4, y: 8 (y_hi: 2, y_lo: 4; y = y_hi * 4 + y_lo), z: 8, core: 2. Of those that a mesh axis runs over, the one named last changes fastest.
Arguments:
- lower_coupling: bfloat16 [4, 4, 2560, 1024], P('layer', None, 'col', 'row'), may hold values from -0.1875 to 0.1875
- upper_inverse: bfloat16 [4, 1024, 1024], P('layer', 'row'), may hold values from -1 to 2, as said below
- upper_coupling: bfloat16 [4, 1024, 10240], P('layer', None, ('row', 'col')), may hold values from -6 to 6
- lower_inverse: bfloat16 [4, 1024, 1024], P('layer'), may hold values from -1 to 1, as said below
- row_pattern: int32 [4, 10240], P('layer'), may hold values 0 or 1
- ancestor_block: bfloat16 [10240, 10240], P(('layer', 'col'), 'row'), may hold values from -6 to 6
Outputs:
- ancestor: bfloat16 [10240, 10240], P(('layer', 'col'), 'row')
The draws below stay inside these ranges and needn't reach their ends.
Inputs may be any that keep to these rules, and one draw needn't show every extreme that they name: `upper_inverse`: zero below the diagonal; diagonal entries between 0.5 and 2. `lower_inverse`: zero above the diagonal; diagonal entries 1.
All inputs are finite; a program needn't handle non-finite values. No bound on the sum of `row_pattern` on one device may be relied on, other than what follows from the above.
Results may differ from the reference program's by a relative error of at most 0.02.
Values may be sent and summed in bfloat16 or wider, within the bound.
No kernel may reach another device: no remote copies, remote signals or barrier semaphores. Data moves between devices by JAX's collectives and lax.ppermute only.
A program may use at most 64 MiB of HBM per device.

```python
import math
import jax
import jax.numpy as jnp
from jax import lax

W = 1024
NF = 10240
LAYERS = 4


def draw_upper_inverse(key, part):
    key = jax.random.fold_in(key, 11)
    key_noise, key_diagonal = jax.random.split(key)
    noise = jnp.clip(jax.random.normal(key_noise, (LAYERS, W, W), jnp.float32), -6.0, 6.0) / math.sqrt(W)
    rows_iota = lax.broadcasted_iota(jnp.int32, (W, W), 0)
    cols_iota = lax.broadcasted_iota(jnp.int32, (W, W), 1)
    above = (cols_iota > rows_iota).astype(jnp.float32)
    identity = (cols_iota == rows_iota).astype(jnp.float32)
    diagonal = jax.random.uniform(key_diagonal, (LAYERS, W), jnp.float32, 0.5, 2.0)
    return (noise * above[None] + diagonal[:, :, None] * identity[None]).astype(jnp.bfloat16)


def draw_lower_inverse(key, part):
    key = jax.random.fold_in(key, 23)
    noise = jnp.clip(jax.random.normal(key, (LAYERS, W, W), jnp.float32), -6.0, 6.0) / math.sqrt(W)
    rows_iota = lax.broadcasted_iota(jnp.int32, (W, W), 0)
    cols_iota = lax.broadcasted_iota(jnp.int32, (W, W), 1)
    below = (cols_iota < rows_iota).astype(jnp.float32)
    identity = (cols_iota == rows_iota).astype(jnp.float32)
    return (noise * below[None] + identity[None]).astype(jnp.bfloat16)


def with_ends(drawn, own_key, least, largest):
    shape = drawn.shape
    spot = [jax.random.randint(jax.random.fold_in(own_key, axis), (), 0, shape[axis]) for axis in range(len(shape))]
    drawn = drawn.at[tuple(spot)].set(least)
    longest = shape.index(max(shape))
    spot[longest] = (spot[longest] + 1) % shape[longest]
    return drawn.at[tuple(spot)].set(largest)


def shard_levels(key, extent, shards, low, largest):
    loudness, own = 1.0, jax.random.fold_in(key, 6)
    for position, parts in shards:
        heights = jnp.exp(jax.random.uniform(jax.random.fold_in(own, position), (parts,), jnp.float32, low / len(shards), largest / len(shards)))
        loudness = loudness * jnp.repeat(heights, extent[position] // parts).reshape([-1 if axis == position else 1 for axis in range(len(extent))])
    return loudness


def normal_values(rng, dims, width, most, shards=(), kind=jnp.bfloat16):
    array = jax.random.normal(rng, dims, jnp.float32) * width
    if len(shards) > 0:
        array = shard_levels(rng, dims, shards, -0.22, 0.18) * array
    return jnp.clip(array, min=-most, max=most).astype(kind)


def setup_inputs(seed: int = 0) -> dict:
    seeds = jax.random.split(jax.random.key(seed), 7)
    lower_coupling = normal_values(seeds[0], (LAYERS, LAYERS, NF // LAYERS, W), W ** -0.5, 0.1875, ((0, 4), (2, 32), (3, 4)))
    upper_inverse = draw_upper_inverse(jax.random.fold_in(seeds[6], 71), 0)
    upper_coupling = normal_values(seeds[2], (LAYERS, W, NF), 1.0, 6.0, ((0, 4), (2, 128)))
    lower_inverse = draw_lower_inverse(jax.random.fold_in(seeds[6], 71), 0)
    row_pattern = with_ends((jax.random.randint(seeds[4], (LAYERS, NF), 0, 4) < 3).astype(jnp.int32), jax.random.fold_in(seeds[4], 1), 0, 1)
    ancestor_block = normal_values(seeds[5], (NF, NF), 1.0, 6.0, ((0, 128), (1, 4)))
    return {"lower_coupling": lower_coupling, "upper_inverse": upper_inverse, "upper_coupling": upper_coupling, "lower_inverse": lower_inverse, "row_pattern": row_pattern, "ancestor_block": ancestor_block}


def reference(lower_coupling, upper_inverse, upper_coupling, lower_inverse, row_pattern, ancestor_block):
    total = jnp.zeros((NF, NF), jnp.float32)
    for layer_number in range(LAYERS):
        coupling = lower_coupling[layer_number].reshape(NF, W)
        pattern = row_pattern[layer_number].astype(jnp.float32)
        lower_panel = jnp.dot(coupling, upper_inverse[layer_number], preferred_element_type=jnp.float32)
        lower_panel = (lower_panel * pattern[:, None]).astype(jnp.bfloat16)
        upper_panel = jnp.dot(lower_inverse[layer_number], upper_coupling[layer_number], preferred_element_type=jnp.float32)
        upper_panel = (upper_panel * pattern[None, :]).astype(jnp.bfloat16)
        contribution = jnp.dot(lower_panel, upper_panel, preferred_element_type=jnp.float32).astype(jnp.bfloat16)
        contribution = lax.optimization_barrier(contribution)
        total = total + contribution.astype(jnp.float32)
    return (ancestor_block.astype(jnp.float32) - total).astype(jnp.bfloat16)
```

```python
import jax
import jax.numpy as jnp
from jax import lax
from jax.sharding import Mesh
from jax.sharding import PartitionSpec as P

AXES = ("layer", "row", "deep", "half", "core")
RING = ("row", "half")


def ring_pairs(step):
    def place(y):
        return (y % 4) * 2 + (y // 4) % 2

    return [(place(y), place((y + step) % 8)) for y in range(8)]


def dot(a, b, contract):
    return lax.dot_general(a, b, (contract, ((), ())), preferred_element_type=jnp.float32)


def shards(
    lower_coupling, upper_inverse, upper_coupling, lower_inverse, row_pattern, ancestor_block
):
    groups, slab_rows = lower_coupling.shape[1:3]
    row_index = lax.axis_index("row")
    deep_index = lax.axis_index("deep")
    half_index = lax.axis_index("half")
    core_index = lax.axis_index("core")
    col_index = deep_index * 4 + half_index * 2 + core_index
    pattern = row_pattern[0].reshape(groups, -1)
    row_mask = lax.dynamic_slice_in_dim(pattern, col_index * slab_rows, slab_rows, 1)
    row_mask = row_mask.reshape(groups * slab_rows, 1).astype(jnp.float32)

    def col_mask(half):
        start = (row_index * 32 + deep_index * 4 + half * 2 + core_index) * slab_rows
        taken = lax.dynamic_slice_in_dim(row_pattern[0], start, slab_rows, 0)
        return taken.reshape(slab_rows, 1).astype(jnp.float32)

    coupling_t = upper_coupling[0].T
    other_coupling_t = lax.ppermute(coupling_t, "half", [(0, 1), (1, 0)])

    def upper_panel(taken, half):
        solved = dot(taken, lower_inverse[0], ((1,), (1,))) * col_mask(half)
        return lax.all_gather(solved.astype(jnp.bfloat16), ("deep", "core"), axis=0, tiled=True)

    upper_own = upper_panel(coupling_t, half_index)
    upper_other = upper_panel(other_coupling_t, 1 - half_index)

    coupling = lower_coupling[0].reshape(groups * slab_rows, -1)
    couplings = [coupling]
    for step in (1, 2, 3):
        pairs = [((r + step) % 4, r) for r in range(4)]
        couplings.append(lax.ppermute(coupling, "row", pairs))
    depth = upper_inverse.shape[1] // 2
    part = lax.dynamic_slice_in_dim(upper_inverse[0], core_index * depth, depth, 0)
    parts = [lax.ppermute(part, RING, ring_pairs(-step)) for step in (1, 2, -1)]
    parts = jnp.concatenate(parts, axis=0)
    other_parts = lax.ppermute(parts, "core", [(0, 1), (1, 0)])
    first = jnp.where(core_index == 0, parts, other_parts)
    second = jnp.where(core_index == 0, other_parts, parts)
    inverses = [upper_inverse[0]]
    for k in range(3):
        inverses.append(first[k * depth : (k + 1) * depth])
        inverses.append(second[k * depth : (k + 1) * depth])
    lower_panel = dot(
        jnp.concatenate(couplings, axis=1), jnp.concatenate(inverses, axis=0), ((1,), (0,))
    )
    lower_panel = (lower_panel * row_mask).astype(jnp.bfloat16)

    def total(panel):
        contribution = dot(lower_panel, panel, ((1,), (1,))).astype(jnp.bfloat16)
        contribution = contribution.reshape(groups, slab_rows, -1)
        arrived = lax.all_to_all(contribution, "layer", 0, 0, tiled=True)
        return jnp.sum(arrived.astype(jnp.float32), axis=0)

    total_own = total(upper_own)
    total_other = total(upper_other)
    low = jnp.where(half_index == 0, total_own, total_other)
    high = jnp.where(half_index == 0, total_other, total_own)
    width = 2 * slab_rows
    strips = []
    for k in range(8):
        strips.append(low[:, k * width : (k + 1) * width])
        strips.append(high[:, k * width : (k + 1) * width])
    summed = jnp.concatenate(strips, axis=1)
    return (ancestor_block.astype(jnp.float32) - summed).astype(jnp.bfloat16)


def solution(mesh):
    fine = Mesh(mesh.devices.reshape(4, 4, 8, 2, 2), AXES)
    col = ("deep", "half", "core")
    placed = (
        P("layer", None, col, "row"),
        P("layer", "row", None),
        P("layer", None, ("row",) + col),
        P("layer", None, None),
        P("layer", None),
        P(("layer",) + col, "row"),
    )
    return jax.shard_map(
        shards, mesh=fine, in_specs=placed, out_specs=P(("layer",) + col, "row"), check_vma=False
    )
```

```python
import jax
import jax.numpy as jnp
from jax import lax
from jax.sharding import Mesh
from jax.sharding import PartitionSpec as P

AXES = ("layer", "row", "deep", "half", "core")
SWAP = [(0, 1), (1, 0)]


def dot(a, b, contract):
    return lax.dot_general(a, b, (contract, ((), ())), preferred_element_type=jnp.float32)


def spread(x, axis):
    copies = jnp.broadcast_to(x[None], (lax.axis_size(axis),) + x.shape)
    return lax.all_to_all(copies, axis, 0, 0, tiled=True)


def shards(
    lower_coupling, upper_inverse, upper_coupling, lower_inverse, row_pattern, ancestor_block
):
    groups, slab_rows = lower_coupling.shape[1:3]
    width = lower_inverse.shape[1]
    row_index = lax.axis_index("row")
    deep_index = lax.axis_index("deep")
    half_index = lax.axis_index("half")
    core_index = lax.axis_index("core")
    col_index = deep_index * 4 + half_index * 2 + core_index

    def mask(start):
        taken = lax.dynamic_slice_in_dim(row_pattern[0], start, slab_rows, 0)
        return taken.reshape(slab_rows, 1).astype(jnp.float32)

    def col_mask(half):
        return mask((row_index * 32 + deep_index * 4 + half * 2 + core_index) * slab_rows)

    def upper_panel(taken, half):
        solved = dot(taken, lower_inverse[0], ((1,), (1,))) * col_mask(half)
        return solved.astype(jnp.bfloat16)

    coupling_t = upper_coupling[0].T
    other_coupling_t = lax.ppermute(coupling_t, "half", SWAP)
    upper_own = lax.all_gather(upper_panel(coupling_t, half_index), "deep", axis=0, tiled=True)
    upper_other = spread(upper_panel(other_coupling_t, 1 - half_index), "deep")
    upper_other = upper_other.reshape(-1, width)

    coupling = lower_coupling[0].reshape(groups * slab_rows, -1)
    partial_value = dot(coupling, upper_inverse[0], ((1,), (0,))).astype(jnp.bfloat16)
    arrived = lax.all_to_all(
        partial_value.reshape(groups, slab_rows, width), "row", 0, 0, tiled=True
    )
    lower_mine = jnp.sum(arrived.astype(jnp.float32), axis=0)
    lower_mine = (lower_mine * mask((row_index * 32 + col_index) * slab_rows)).astype(jnp.bfloat16)
    lower_panel = spread(lower_mine, "row")
    lower_other = lax.ppermute(lower_panel, "core", SWAP)
    first = jnp.where(core_index == 0, lower_panel, lower_other)
    second = jnp.where(core_index == 0, lower_other, lower_panel)
    lower_panel = jnp.stack([first, second], axis=1).reshape(-1, width)

    def total(panel):
        contribution = dot(lower_panel, panel, ((1,), (1,))).astype(jnp.bfloat16)
        contribution = contribution.reshape(groups * 2, slab_rows, -1)
        arrived = lax.all_to_all(contribution, ("layer", "core"), 0, 0, tiled=True)
        arrived = arrived.reshape((groups, 2) + arrived.shape[1:])
        return jnp.sum(arrived.astype(jnp.float32), axis=0)

    total_own = total(upper_own)
    total_other = total(upper_other)
    low = jnp.where(half_index == 0, total_own, total_other)
    high = jnp.where(half_index == 0, total_other, total_own)
    strips = []
    for k in range(8):
        here = slice(k * slab_rows, (k + 1) * slab_rows)
        strips += [low[0, :, here], low[1, :, here], high[0, :, here], high[1, :, here]]
    summed = jnp.concatenate(strips, axis=1)
    return (ancestor_block.astype(jnp.float32) - summed).astype(jnp.bfloat16)


def solution(mesh):
    fine = Mesh(mesh.devices.reshape(4, 4, 8, 2, 2), AXES)
    col = ("deep", "half", "core")
    placed = (
        P("layer", None, col, "row"),
        P("layer", "row", None),
        P("layer", None, ("row",) + col),
        P("layer", None, None),
        P("layer", None),
        P(("layer",) + col, "row"),
    )
    return jax.shard_map(
        shards, mesh=fine, in_specs=placed, out_specs=P(("layer",) + col, "row"), check_vma=False
    )
```

```python
import jax
import jax.numpy as jnp
from jax import lax
from jax.experimental import pallas as pl
from jax.experimental.pallas import tpu as pltpu
from jax.sharding import Mesh
from jax.sharding import PartitionSpec as P

AXES = ("layer", "row", "deep", "half", "core")
SWAP = [(0, 1), (1, 0)]
STEPS = (2, 1, 3, 0)
PIECES = 4


def turn(size, step):
    return [(i, (i + step) % size) for i in range(size)]


def dot(a, b, contract):
    return lax.dot_general(a, b, (contract, ((), ())), preferred_element_type=jnp.float32)


def spread(x, axis):
    copies = jnp.broadcast_to(x[None], (lax.axis_size(axis),) + x.shape)
    return lax.all_to_all(copies, axis, 0, 0, tiled=True)


def multiply_kernel(place, lower, upper, out2, out1, out3, out0, rows, panel):
    strip = lower.shape[1]

    @pl.when(pl.program_id(0) == 0)
    def _():
        for k, step in enumerate(STEPS):
            rows[k * strip : (k + 1) * strip, :] = lower[place[step]]

    half = place[len(STEPS)]
    for z in range(panel.shape[0] // (4 * strip)):
        for core in range(2):
            start = (4 * z + 2 * core) * strip
            own = upper[start : start + strip, :]
            far = upper[start + strip : start + 2 * strip, :]
            low = (4 * z + core) * strip
            panel[low : low + strip, :] = jnp.where(half == 0, own, far)
            panel[low + 2 * strip : low + 3 * strip, :] = jnp.where(half == 0, far, own)
    value = dot(rows[...], panel[...], ((1,), (1,))).astype(out0.dtype)
    for k, out in enumerate((out2, out1, out3, out0)):
        out[...] = value[k * strip : (k + 1) * strip, :]


def multiply(place, lower, upper):
    strip, width = lower.shape[1:]
    columns = upper.shape[0]
    piece = columns // PIECES
    out = pl.BlockSpec((strip, piece), lambda i: (0, i))
    return pl.pallas_call(
        multiply_kernel,
        grid=(PIECES,),
        out_shape=(jax.ShapeDtypeStruct((strip, columns), jnp.bfloat16),) * len(STEPS),
        in_specs=[
            pl.BlockSpec(memory_space=pltpu.SMEM),
            pl.BlockSpec(lower.shape, lambda i: (0, 0, 0)),
            pl.BlockSpec((piece, width), lambda i: (i, 0)),
        ],
        out_specs=(out,) * len(STEPS),
        scratch_shapes=[
            pltpu.VMEM((len(STEPS) * strip, width), jnp.bfloat16),
            pltpu.VMEM((piece, width), jnp.bfloat16),
        ],
        compiler_params=pltpu.CompilerParams(vmem_limit_bytes=60 << 20),
    )(place, lower, upper)


def shards(
    lower_coupling, upper_inverse, upper_coupling, lower_inverse, row_pattern, ancestor_block
):
    groups, slab_rows = lower_coupling.shape[1:3]
    width = lower_inverse.shape[1]
    layer_index = lax.axis_index("layer")
    row_index = lax.axis_index("row")
    half_index = lax.axis_index("half")
    pair_index = lax.axis_index("deep") * 4 + lax.axis_index("core")

    def mask(start):
        taken = lax.dynamic_slice_in_dim(row_pattern[0], start * slab_rows, slab_rows, 0)
        return taken.reshape(slab_rows, 1).astype(jnp.float32)

    def upper_panel(taken, half):
        solved = dot(taken, lower_inverse[0], ((1,), (1,)))
        solved = solved * mask(row_index * 32 + pair_index + half * 2)
        return solved.astype(jnp.bfloat16)

    coupling_t = upper_coupling[0].T
    other_coupling_t = lax.ppermute(coupling_t, "half", SWAP)
    solved_own = upper_panel(coupling_t, half_index)
    solved_other = upper_panel(other_coupling_t, 1 - half_index)
    solved = jnp.concatenate([solved_own, solved_other], axis=0)
    upper = lax.all_gather(solved, ("deep", "core"), axis=0, tiled=True)

    coupling = lower_coupling[0].reshape(groups * slab_rows, -1)
    partial_value = dot(coupling, upper_inverse[0], ((1,), (0,))).astype(jnp.bfloat16)
    arrived = lax.all_to_all(
        partial_value.reshape(groups, slab_rows, width), "row", 0, 0, tiled=True
    )
    arrived, solved = lax.optimization_barrier((arrived, solved))
    lower_mine = jnp.sum(arrived.astype(jnp.float32), axis=0)
    lower_mine = lower_mine * mask(row_index * 32 + pair_index + half_index * 2)
    lower_panel = spread(lower_mine.astype(jnp.bfloat16), "row")

    targets = (layer_index + jnp.arange(groups)) % groups
    place = jnp.concatenate([targets, half_index[None]]).astype(jnp.int32)
    total = jnp.zeros((), jnp.float32)
    for step, part in zip(STEPS, multiply(place, lower_panel, upper)):
        if step:
            part = lax.ppermute(part, "layer", turn(groups, step))
        total = total + part.astype(jnp.float32)
    return (ancestor_block.astype(jnp.float32) - total).astype(jnp.bfloat16)


def solution(mesh):
    fine = Mesh(mesh.devices.reshape(4, 4, 8, 2, 2), AXES)
    col = ("deep", "half", "core")
    placed = (
        P("layer", None, col, "row"),
        P("layer", "row", None),
        P("layer", None, ("row",) + col),
        P("layer", None, None),
        P("layer", None),
        P(("layer",) + col, "row"),
    )
    return jax.shard_map(
        shards, mesh=fine, in_specs=placed, out_specs=P(("layer",) + col, "row"), check_vma=False
    )
```

```python
import jax
import jax.numpy as jnp
from jax import lax
from jax.experimental import pallas as pl
from jax.experimental.pallas import tpu as pltpu
from jax.sharding import Mesh
from jax.sharding import PartitionSpec as P

AXES = ("layer", "row", "deep", "half", "core")
SWAP = [(0, 1), (1, 0)]
PIECES = 4
SHARES = 4
MULTIPLY_VMEM = 48 << 20


def layer_pairs(step):
    pairs = []
    for x in range(4):
        pairs.append((x * 2, (x + step) % 4 * 2))
        pairs.append((x * 2 + 1, (x - step) % 4 * 2 + 1))
    return pairs


def dot(a, b, contract):
    return lax.dot_general(a, b, (contract, ((), ())), preferred_element_type=jnp.float32)


def spread(x, axis):
    copies = jnp.broadcast_to(x[None], (lax.axis_size(axis),) + x.shape)
    return lax.all_to_all(copies, axis, 0, 0, tiled=True)


def join_kernel(own, far, out):
    rows = own.shape[0]
    out[:rows, :] = own[...]
    out[rows:, :] = far[...]


def join(own, far):
    rows, width = own.shape
    vmem = pl.BlockSpec(memory_space=pltpu.VMEM)
    return pl.pallas_call(
        join_kernel,
        out_shape=jax.ShapeDtypeStruct((2 * rows, width), own.dtype),
        in_specs=[vmem] * 2,
        out_specs=vmem,
        compiler_params=pltpu.CompilerParams(vmem_limit_bytes=32 << 20),
    )(own, far)


def multiply_kernel(place, mask, lower, *refs):
    uppers, outs, (rows, panel) = refs[:SHARES], refs[SHARES:-2], refs[-2:]
    strip = lower.shape[1]

    @pl.when(pl.program_id(0) == 0)
    def _():
        for k in range(4):
            rows[k * strip : (k + 1) * strip, :] = lower[place[k]]

    half = place[4]
    share = uppers[0].shape[0] // strip
    for n in range(SHARES * share):
        z, core, k = n // 4, n // 2 % 2, n % 2
        to = (4 * z + core) * strip + jnp.where(half == k, 0, 2 * strip)
        block = uppers[n // share][n % share * strip : (n % share + 1) * strip, :]
        panel[pl.ds(pl.multiple_of(to, 16), strip), :] = block
    value = (dot(rows[...], panel[...], ((1,), (1,))) * mask[...]).astype(jnp.bfloat16)
    for k, out in enumerate(outs):
        out[...] = value[k * strip : (k + 1) * strip, :]


def multiply(place, mask, lower, upper):
    groups, strip, width = lower.shape
    columns = upper.shape[0]
    piece = columns // PIECES
    out = pl.BlockSpec((strip, piece), lambda i: (0, i))
    shares = [
        pl.BlockSpec((piece // SHARES, width), lambda i, k=k: (i * SHARES + k, 0))
        for k in range(SHARES)
    ]
    return pl.pallas_call(
        multiply_kernel,
        grid=(PIECES,),
        out_shape=(jax.ShapeDtypeStruct((strip, columns), jnp.bfloat16),) * groups,
        in_specs=[
            pl.BlockSpec(memory_space=pltpu.SMEM),
            pl.BlockSpec((1, piece), lambda i: (0, i)),
            pl.BlockSpec(lower.shape, lambda i: (0, 0, 0)),
        ] + shares,
        out_specs=(out,) * groups,
        scratch_shapes=[
            pltpu.VMEM((groups * strip, width), jnp.bfloat16),
            pltpu.VMEM((piece, width), jnp.bfloat16),
        ],
        compiler_params=pltpu.CompilerParams(vmem_limit_bytes=MULTIPLY_VMEM),
    )(place, mask, lower, *([upper] * SHARES))


def shards(
    lower_coupling, upper_inverse, upper_coupling, lower_inverse, row_pattern, ancestor_block
):
    groups, slab_rows = lower_coupling.shape[1:3]
    width = lower_inverse.shape[1]
    layer_index = lax.axis_index("layer")
    row_index = lax.axis_index("row")
    half_index = lax.axis_index("half")
    deep_index = lax.axis_index("deep")
    core_index = lax.axis_index("core")
    slab = ((row_index * 8 + deep_index) * 2 + half_index) * 2 + core_index

    coupling_t = upper_coupling[0].T
    other = lax.ppermute(coupling_t, "half", SWAP)
    solver = dot(upper_inverse[0], lower_inverse[0], ((1,), (0,))).astype(jnp.bfloat16)
    coupling = lower_coupling[0].reshape(groups * slab_rows, -1)
    partial_value = dot(coupling, solver, ((1,), (0,))).astype(jnp.bfloat16)
    other, partial_value = lax.optimization_barrier((other, partial_value))
    both = join(coupling_t, other)
    upper = lax.all_gather(both, ("deep", "core"), axis=0, tiled=True)
    partial_value, both = lax.optimization_barrier((partial_value, both))
    arrived = lax.all_to_all(
        partial_value.reshape(groups, slab_rows, width), "row", 0, 0, tiled=True
    )
    row_mask = lax.dynamic_slice_in_dim(row_pattern[0], slab * slab_rows, slab_rows, 0)
    row_mask = row_mask.reshape(slab_rows, 1).astype(jnp.float32)
    lower_mine = jnp.sum(arrived.astype(jnp.float32), axis=0) * row_mask
    lower_panel = spread(lower_mine.astype(jnp.bfloat16), "row")
    mask = lax.dynamic_slice_in_dim(
        row_pattern[0], row_index * (groups * 8 * slab_rows), groups * 8 * slab_rows, 0
    )
    mask = mask.reshape(1, -1).astype(jnp.float32)

    onward = jnp.where(core_index == 0, 1, 3)
    targets = (layer_index + jnp.stack([2 * onward, 3 * onward, onward, 0 * onward])) % groups
    place = jnp.concatenate([targets, half_index[None]]).astype(jnp.int32)
    across, back, near, kept = multiply(place, mask, lower_panel, upper)
    across = lax.ppermute(across, ("layer", "core"), layer_pairs(1))
    back = lax.ppermute(back, ("layer", "core"), layer_pairs(-1))
    near = (near.astype(jnp.float32) + across.astype(jnp.float32)).astype(jnp.bfloat16)
    near = lax.ppermute(near, ("layer", "core"), layer_pairs(1))
    total = kept.astype(jnp.float32) + back.astype(jnp.float32) + near.astype(jnp.float32)
    return (ancestor_block.astype(jnp.float32) - total).astype(jnp.bfloat16)


def solution(mesh):
    fine = Mesh(mesh.devices.reshape(4, 4, 8, 2, 2), AXES)
    col = ("deep", "half", "core")
    placed = (
        P("layer", None, col, "row"),
        P("layer", "row", None),
        P("layer", None, ("row",) + col),
        P("layer", None, None),
        P("layer", None),
        P(("layer",) + col, "row"),
    )
    return jax.shard_map(
        shards, mesh=fine, in_specs=placed, out_specs=P(("layer",) + col, "row"), check_vma=False
    )
```

```python
import jax
import jax.numpy as jnp
from jax import lax
from jax.experimental import pallas as pl
from jax.experimental.pallas import tpu as pltpu
from jax.sharding import Mesh
from jax.sharding import PartitionSpec as P

AXES = ("layer", "row", "deep", "half", "core")
SWAP = [(0, 1), (1, 0)]
PIECES = 4
SHARES = 4
MULTIPLY_VMEM = 48 << 20


def layer_pairs(step):
    pairs = []
    for x in range(4):
        pairs.append((x * 2, (x + step) % 4 * 2))
        pairs.append((x * 2 + 1, (x - step) % 4 * 2 + 1))
    return pairs


def dot(a, b, contract):
    return lax.dot_general(a, b, (contract, ((), ())), preferred_element_type=jnp.float32)


def spread(x, axis):
    copies = jnp.broadcast_to(x[None], (lax.axis_size(axis),) + x.shape)
    return lax.all_to_all(copies, axis, 0, 0, tiled=True)


def join_kernel(own, far, out):
    rows = own.shape[0]
    out[:rows, :] = own[...]
    out[rows:, :] = far[...]


def join(own, far):
    rows, width = own.shape
    vmem = pl.BlockSpec(memory_space=pltpu.VMEM)
    return pl.pallas_call(
        join_kernel,
        out_shape=jax.ShapeDtypeStruct((2 * rows, width), own.dtype),
        in_specs=[vmem] * 2,
        out_specs=vmem,
        compiler_params=pltpu.CompilerParams(vmem_limit_bytes=32 << 20),
    )(own, far)


def multiply_kernel(place, mask, lower, *refs):
    uppers, outs, (rows, panel) = refs[:SHARES], refs[SHARES:-2], refs[-2:]
    strip = lower.shape[1]

    @pl.when(pl.program_id(0) == 0)
    def _():
        for k in range(4):
            rows[k * strip : (k + 1) * strip, :] = lower[place[k]]

    half = place[4]
    share = uppers[0].shape[0] // strip
    for n in range(SHARES * share):
        z, core, k = n // 4, n // 2 % 2, n % 2
        to = (4 * z + core) * strip + jnp.where(half == k, 0, 2 * strip)
        block = uppers[n // share][n % share * strip : (n % share + 1) * strip, :]
        panel[pl.ds(pl.multiple_of(to, 16), strip), :] = block
    value = (dot(rows[...], panel[...], ((1,), (1,))) * mask[...]).astype(jnp.bfloat16)
    across_a, across_b, near_a, near_b, back, kept = outs

    @pl.when(pl.program_id(0) < PIECES // 2)
    def _():
        across_a[...] = value[:strip, :]
        near_a[...] = value[2 * strip : 3 * strip, :]

    @pl.when(pl.program_id(0) >= PIECES // 2)
    def _():
        across_b[...] = value[:strip, :]
        near_b[...] = value[2 * strip : 3 * strip, :]

    back[...] = value[strip : 2 * strip, :]
    kept[...] = value[3 * strip :, :]


def multiply(place, mask, lower, upper):
    groups, strip, width = lower.shape
    columns = upper.shape[0]
    piece = columns // PIECES
    half = PIECES // 2
    out = pl.BlockSpec((strip, piece), lambda i: (0, i))
    first = pl.BlockSpec((strip, piece), lambda i: (0, jnp.minimum(i, half - 1)))
    second = pl.BlockSpec((strip, piece), lambda i: (0, jnp.maximum(i - half, 0)))
    part = jax.ShapeDtypeStruct((strip, columns // 2), jnp.bfloat16)
    whole = jax.ShapeDtypeStruct((strip, columns), jnp.bfloat16)
    shares = [
        pl.BlockSpec((piece // SHARES, width), lambda i, k=k: (i * SHARES + k, 0))
        for k in range(SHARES)
    ]
    return pl.pallas_call(
        multiply_kernel,
        grid=(PIECES,),
        out_shape=(part,) * 4 + (whole,) * 2,
        in_specs=[
            pl.BlockSpec(memory_space=pltpu.SMEM),
            pl.BlockSpec((1, piece), lambda i: (0, i)),
            pl.BlockSpec(lower.shape, lambda i: (0, 0, 0)),
        ] + shares,
        out_specs=(first, second, first, second, out, out),
        scratch_shapes=[
            pltpu.VMEM((groups * strip, width), jnp.bfloat16),
            pltpu.VMEM((piece, width), jnp.bfloat16),
        ],
        compiler_params=pltpu.CompilerParams(vmem_limit_bytes=MULTIPLY_VMEM),
    )(place, mask, lower, *([upper] * SHARES))


def shards(
    lower_coupling, upper_inverse, upper_coupling, lower_inverse, row_pattern, ancestor_block
):
    groups, slab_rows = lower_coupling.shape[1:3]
    width = lower_inverse.shape[1]
    layer_index = lax.axis_index("layer")
    row_index = lax.axis_index("row")
    half_index = lax.axis_index("half")
    deep_index = lax.axis_index("deep")
    core_index = lax.axis_index("core")
    slab = ((row_index * 8 + deep_index) * 2 + half_index) * 2 + core_index

    coupling_t = upper_coupling[0].T
    other = lax.ppermute(coupling_t, "half", SWAP)
    solver = dot(upper_inverse[0], lower_inverse[0], ((1,), (0,))).astype(jnp.bfloat16)
    coupling = lower_coupling[0].reshape(groups * slab_rows, -1)
    partial_value = dot(coupling, solver, ((1,), (0,))).astype(jnp.bfloat16)
    other, partial_value = lax.optimization_barrier((other, partial_value))
    both = join(coupling_t, other)
    upper = lax.all_gather(both, ("deep", "core"), axis=0, tiled=True)
    partial_value, both = lax.optimization_barrier((partial_value, both))
    arrived = lax.all_to_all(
        partial_value.reshape(groups, slab_rows, width), "row", 0, 0, tiled=True
    )
    row_mask = lax.dynamic_slice_in_dim(row_pattern[0], slab * slab_rows, slab_rows, 0)
    row_mask = row_mask.reshape(slab_rows, 1).astype(jnp.float32)
    lower_mine = jnp.sum(arrived.astype(jnp.float32), axis=0) * row_mask
    lower_panel = spread(lower_mine.astype(jnp.bfloat16), "row")
    mask = lax.dynamic_slice_in_dim(
        row_pattern[0], row_index * (groups * 8 * slab_rows), groups * 8 * slab_rows, 0
    )
    mask = mask.reshape(1, -1).astype(jnp.float32)

    onward = jnp.where(core_index == 0, 1, 3)
    targets = (layer_index + jnp.stack([2 * onward, 3 * onward, onward, 0 * onward])) % groups
    place = jnp.concatenate([targets, half_index[None]]).astype(jnp.int32)
    across_a, across_b, near_a, near_b, back, kept = multiply(place, mask, lower_panel, upper)
    across = [lax.ppermute(part, ("layer", "core"), layer_pairs(1)) for part in (across_a, across_b)]
    back = lax.ppermute(back, ("layer", "core"), layer_pairs(-1))
    total = kept.astype(jnp.float32) + back.astype(jnp.float32)
    total = ancestor_block.astype(jnp.float32) - total
    halves = []
    for k, (near, part) in enumerate(zip((near_a, near_b), across)):
        near = (near.astype(jnp.float32) + part.astype(jnp.float32)).astype(jnp.bfloat16)
        near = lax.ppermute(near, ("layer", "core"), layer_pairs(1))
        columns = near.shape[1]
        halves.append(total[:, k * columns : (k + 1) * columns] - near.astype(jnp.float32))
    return jnp.concatenate(halves, axis=1).astype(jnp.bfloat16)


def solution(mesh):
    fine = Mesh(mesh.devices.reshape(4, 4, 8, 2, 2), AXES)
    col = ("deep", "half", "core")
    placed = (
        P("layer", None, col, "row"),
        P("layer", "row", None),
        P("layer", None, ("row",) + col),
        P("layer", None, None),
        P("layer", None),
        P(("layer",) + col, "row"),
    )
    return jax.shard_map(
        shards, mesh=fine, in_specs=placed, out_specs=P(("layer",) + col, "row"), check_vma=False
    )
```

```python
import jax
import jax.numpy as jnp
from jax import lax
from jax.experimental import pallas as pl
from jax.experimental.pallas import tpu as pltpu
from jax.sharding import Mesh
from jax.sharding import PartitionSpec as P

AXES = ("layer", "row", "deep", "half", "core")
SWAP = [(0, 1), (1, 0)]
PIECES = 2
SHARES = 4
MULTIPLY_VMEM = 48 << 20


def layer_pairs(step):
    pairs = []
    for x in range(4):
        pairs.append((x * 2, (x + step) % 4 * 2))
        pairs.append((x * 2 + 1, (x - step) % 4 * 2 + 1))
    return pairs


def dot(a, b, contract):
    return lax.dot_general(a, b, (contract, ((), ())), preferred_element_type=jnp.float32)


def spread(x, axis):
    copies = jnp.broadcast_to(x[None], (lax.axis_size(axis),) + x.shape)
    return lax.all_to_all(copies, axis, 0, 0, tiled=True)


def join_kernel(own, far, out):
    rows = own.shape[0]
    out[:rows, :] = own[...]
    out[rows:, :] = far[...]


def join(own, far):
    rows, width = own.shape
    vmem = pl.BlockSpec(memory_space=pltpu.VMEM)
    return pl.pallas_call(
        join_kernel,
        out_shape=jax.ShapeDtypeStruct((2 * rows, width), own.dtype),
        in_specs=[vmem] * 2,
        out_specs=vmem,
        compiler_params=pltpu.CompilerParams(vmem_limit_bytes=32 << 20),
    )(own, far)


def multiply_kernel(place, mask, lower, *refs):
    uppers, outs, (rows, panel) = refs[:SHARES], refs[SHARES:-2], refs[-2:]
    strip = lower.shape[1]

    @pl.when(pl.program_id(0) == 0)
    def _():
        for k in range(4):
            rows[k * strip : (k + 1) * strip, :] = lower[place[k]]

    half = place[4]
    share = uppers[0].shape[0] // strip
    for n in range(SHARES * share):
        z, core, k = n // 4, n // 2 % 2, n % 2
        to = (4 * z + core) * strip + jnp.where(half == k, 0, 2 * strip)
        block = uppers[n // share][n % share * strip : (n % share + 1) * strip, :]
        panel[pl.ds(pl.multiple_of(to, 16), strip), :] = block
    value = (dot(rows[...], panel[...], ((1,), (1,))) * mask[...]).astype(jnp.bfloat16)
    across_a, across_b, near_a, near_b, back, kept = outs

    @pl.when(pl.program_id(0) < PIECES // 2)
    def _():
        across_a[...] = value[:strip, :]
        near_a[...] = value[2 * strip : 3 * strip, :]

    @pl.when(pl.program_id(0) >= PIECES // 2)
    def _():
        across_b[...] = value[:strip, :]
        near_b[...] = value[2 * strip : 3 * strip, :]

    back[...] = value[strip : 2 * strip, :]
    kept[...] = value[3 * strip :, :]


def multiply(place, mask, lower, upper):
    groups, strip, width = lower.shape
    columns = upper.shape[0]
    piece = columns // PIECES
    half = PIECES // 2
    out = pl.BlockSpec((strip, piece), lambda i: (0, i))
    first = pl.BlockSpec((strip, piece), lambda i: (0, jnp.minimum(i, half - 1)))
    second = pl.BlockSpec((strip, piece), lambda i: (0, jnp.maximum(i - half, 0)))
    part = jax.ShapeDtypeStruct((strip, columns // 2), jnp.bfloat16)
    whole = jax.ShapeDtypeStruct((strip, columns), jnp.bfloat16)
    shares = [
        pl.BlockSpec((piece // SHARES, width), lambda i, k=k: (i * SHARES + k, 0))
        for k in range(SHARES)
    ]
    return pl.pallas_call(
        multiply_kernel,
        grid=(PIECES,),
        out_shape=(part,) * 4 + (whole,) * 2,
        in_specs=[
            pl.BlockSpec(memory_space=pltpu.SMEM),
            pl.BlockSpec((1, piece), lambda i: (0, i)),
            pl.BlockSpec(lower.shape, lambda i: (0, 0, 0)),
        ] + shares,
        out_specs=(first, second, first, second, out, out),
        scratch_shapes=[
            pltpu.VMEM((groups * strip, width), jnp.bfloat16),
            pltpu.VMEM((piece, width), jnp.bfloat16),
        ],
        compiler_params=pltpu.CompilerParams(vmem_limit_bytes=MULTIPLY_VMEM),
    )(place, mask, lower, *([upper] * SHARES))


def shards(
    lower_coupling, upper_inverse, upper_coupling, lower_inverse, row_pattern, ancestor_block
):
    groups, slab_rows = lower_coupling.shape[1:3]
    width = lower_inverse.shape[1]
    layer_index = lax.axis_index("layer")
    row_index = lax.axis_index("row")
    half_index = lax.axis_index("half")
    deep_index = lax.axis_index("deep")
    core_index = lax.axis_index("core")
    slab = ((row_index * 8 + deep_index) * 2 + half_index) * 2 + core_index

    coupling_t = upper_coupling[0].T
    other = lax.ppermute(coupling_t, "half", SWAP)
    solver = dot(upper_inverse[0], lower_inverse[0], ((1,), (0,))).astype(jnp.bfloat16)
    coupling = lower_coupling[0].reshape(groups * slab_rows, -1)
    partial_value = dot(coupling, solver, ((1,), (0,))).astype(jnp.bfloat16)
    other, partial_value = lax.optimization_barrier((other, partial_value))
    both = join(coupling_t, other)
    upper = lax.all_gather(both, ("deep", "core"), axis=0, tiled=True)
    partial_value, both = lax.optimization_barrier((partial_value, both))
    arrived = lax.all_to_all(
        partial_value.reshape(groups, slab_rows, width), "row", 0, 0, tiled=True
    )
    row_mask = lax.dynamic_slice_in_dim(row_pattern[0], slab * slab_rows, slab_rows, 0)
    row_mask = row_mask.reshape(slab_rows, 1).astype(jnp.float32)
    lower_mine = jnp.sum(arrived.astype(jnp.float32), axis=0) * row_mask
    lower_panel = spread(lower_mine.astype(jnp.bfloat16), "row")
    mask = lax.dynamic_slice_in_dim(
        row_pattern[0], row_index * (groups * 8 * slab_rows), groups * 8 * slab_rows, 0
    )
    mask = mask.reshape(1, -1).astype(jnp.float32)

    onward = jnp.where(core_index == 0, 1, 3)
    targets = (layer_index + jnp.stack([2 * onward, 3 * onward, onward, 0 * onward])) % groups
    place = jnp.concatenate([targets, half_index[None]]).astype(jnp.int32)
    across_a, across_b, near_a, near_b, back, kept = multiply(place, mask, lower_panel, upper)
    across = [lax.ppermute(part, ("layer", "core"), layer_pairs(1)) for part in (across_a, across_b)]
    back = lax.ppermute(back, ("layer", "core"), layer_pairs(-1))
    total = kept.astype(jnp.float32) + back.astype(jnp.float32)
    total = ancestor_block.astype(jnp.float32) - total
    halves = []
    for k, (near, part) in enumerate(zip((near_a, near_b), across)):
        near = (near.astype(jnp.float32) + part.astype(jnp.float32)).astype(jnp.bfloat16)
        near = lax.ppermute(near, ("layer", "core"), layer_pairs(1))
        columns = near.shape[1]
        halves.append(total[:, k * columns : (k + 1) * columns] - near.astype(jnp.float32))
    return jnp.concatenate(halves, axis=1).astype(jnp.bfloat16)


def solution(mesh):
    fine = Mesh(mesh.devices.reshape(4, 4, 8, 2, 2), AXES)
    col = ("deep", "half", "core")
    placed = (
        P("layer", None, col, "row"),
        P("layer", "row", None),
        P("layer", None, ("row",) + col),
        P("layer", None, None),
        P("layer", None),
        P(("layer",) + col, "row"),
    )
    return jax.shard_map(
        shards, mesh=fine, in_specs=placed, out_specs=P(("layer",) + col, "row"), check_vma=False
    )
```

```python
import functools

import jax
import jax.numpy as jnp
from jax import lax
from jax.experimental import pallas as pl
from jax.experimental.pallas import tpu as pltpu
from jax.sharding import Mesh
from jax.sharding import PartitionSpec as P

AXES = ("layer", "row", "deep", "half", "core")
SWAP = [(0, 1), (1, 0)]
PIECES = 2
SHARES = 4
MULTIPLY_VMEM = 48 << 20


def layer_pairs(step):
    pairs = []
    for x in range(4):
        pairs.append((x * 2, (x + step) % 4 * 2))
        pairs.append((x * 2 + 1, (x - step) % 4 * 2 + 1))
    return pairs


def dot(a, b, contract):
    return lax.dot_general(a, b, (contract, ((), ())), preferred_element_type=jnp.float32)


def spread(x, axis):
    copies = jnp.broadcast_to(x[None], (lax.axis_size(axis),) + x.shape)
    return lax.all_to_all(copies, axis, 0, 0, tiled=True)


def join_kernel(own, far, out):
    rows = own.shape[0]
    out[:rows, :] = own[...]
    out[rows:, :] = far[...]


def join(own, far):
    rows, width = own.shape
    vmem = pl.BlockSpec(memory_space=pltpu.VMEM)
    return pl.pallas_call(
        join_kernel,
        out_shape=jax.ShapeDtypeStruct((2 * rows, width), own.dtype),
        in_specs=[vmem] * 2,
        out_specs=vmem,
        compiler_params=pltpu.CompilerParams(vmem_limit_bytes=32 << 20),
    )(own, far)


def multiply_kernel(first, place, mask, lower, *refs):
    uppers, outs, (rows, panel) = refs[:SHARES], refs[SHARES:-2], refs[-2:]
    strip = lower.shape[1]

    @pl.when(pl.program_id(0) == 0)
    def _():
        for k in range(rows.shape[0] // strip):
            rows[k * strip : (k + 1) * strip, :] = lower[place[first + k]]

    half = place[4]
    share = uppers[0].shape[0] // strip
    for n in range(SHARES * share):
        z, core, k = n // 4, n // 2 % 2, n % 2
        to = (4 * z + core) * strip + jnp.where(half == k, 0, 2 * strip)
        block = uppers[n // share][n % share * strip : (n % share + 1) * strip, :]
        panel[pl.ds(pl.multiple_of(to, 16), strip), :] = block
    value = (dot(rows[...], panel[...], ((1,), (1,))) * mask[...]).astype(jnp.bfloat16)
    if first:
        outs[0][...] = value
        return
    across_a, across_b, near_a, near_b, back = outs

    @pl.when(pl.program_id(0) < PIECES // 2)
    def _():
        across_a[...] = value[:strip, :]
        near_a[...] = value[2 * strip : 3 * strip, :]

    @pl.when(pl.program_id(0) >= PIECES // 2)
    def _():
        across_b[...] = value[:strip, :]
        near_b[...] = value[2 * strip : 3 * strip, :]

    back[...] = value[strip : 2 * strip, :]


def multiply(kept, place, mask, lower, upper):
    groups, strip, width = lower.shape
    columns = upper.shape[0]
    piece = columns // PIECES
    half = PIECES // 2
    out = pl.BlockSpec((strip, piece), lambda i: (0, i))
    first = pl.BlockSpec((strip, piece), lambda i: (0, jnp.minimum(i, half - 1)))
    second = pl.BlockSpec((strip, piece), lambda i: (0, jnp.maximum(i - half, 0)))
    part = jax.ShapeDtypeStruct((strip, columns // 2), jnp.bfloat16)
    whole = jax.ShapeDtypeStruct((strip, columns), jnp.bfloat16)
    shares = [
        pl.BlockSpec((piece // SHARES, width), lambda i, k=k: (i * SHARES + k, 0))
        for k in range(SHARES)
    ]
    return pl.pallas_call(
        functools.partial(multiply_kernel, 3 if kept else 0),
        grid=(PIECES,),
        out_shape=(whole,) if kept else (part,) * 4 + (whole,),
        in_specs=[
            pl.BlockSpec(memory_space=pltpu.SMEM),
            pl.BlockSpec((1, piece), lambda i: (0, i)),
            pl.BlockSpec(lower.shape, lambda i: (0, 0, 0)),
        ] + shares,
        out_specs=(out,) if kept else (first, second, first, second, out),
        scratch_shapes=[
            pltpu.VMEM(((1 if kept else 3) * strip, width), jnp.bfloat16),
            pltpu.VMEM((piece, width), jnp.bfloat16),
        ],
        compiler_params=pltpu.CompilerParams(vmem_limit_bytes=MULTIPLY_VMEM),
    )(place, mask, lower, *([upper] * SHARES))


def shards(
    lower_coupling, upper_inverse, upper_coupling, lower_inverse, row_pattern, ancestor_block
):
    groups, slab_rows = lower_coupling.shape[1:3]
    width = lower_inverse.shape[1]
    layer_index = lax.axis_index("layer")
    row_index = lax.axis_index("row")
    half_index = lax.axis_index("half")
    deep_index = lax.axis_index("deep")
    core_index = lax.axis_index("core")
    slab = ((row_index * 8 + deep_index) * 2 + half_index) * 2 + core_index

    coupling_t = upper_coupling[0].T
    other = lax.ppermute(coupling_t, "half", SWAP)
    solver = dot(upper_inverse[0], lower_inverse[0], ((1,), (0,))).astype(jnp.bfloat16)
    coupling = lower_coupling[0].reshape(groups * slab_rows, -1)
    partial_value = dot(coupling, solver, ((1,), (0,))).astype(jnp.bfloat16)
    other, partial_value = lax.optimization_barrier((other, partial_value))
    both = join(coupling_t, other)
    upper = lax.all_gather(both, ("deep", "core"), axis=0, tiled=True)
    arrived = lax.all_to_all(
        partial_value.reshape(groups, slab_rows, width), "row", 0, 0, tiled=True
    )
    row_mask = lax.dynamic_slice_in_dim(row_pattern[0], slab * slab_rows, slab_rows, 0)
    row_mask = row_mask.reshape(slab_rows, 1).astype(jnp.float32)
    lower_mine = jnp.sum(arrived.astype(jnp.float32), axis=0) * row_mask
    lower_panel = spread(lower_mine.astype(jnp.bfloat16), "row")
    mask = lax.dynamic_slice_in_dim(
        row_pattern[0], row_index * (groups * 8 * slab_rows), groups * 8 * slab_rows, 0
    )
    mask = mask.reshape(1, -1).astype(jnp.float32)

    onward = jnp.where(core_index == 0, 1, 3)
    targets = (layer_index + jnp.stack([2 * onward, 3 * onward, onward, 0 * onward])) % groups
    place = jnp.concatenate([targets, half_index[None]]).astype(jnp.int32)
    across_a, across_b, near_a, near_b, back = multiply(False, place, mask, lower_panel, upper)
    across = [lax.ppermute(part, ("layer", "core"), layer_pairs(1)) for part in (across_a, across_b)]
    back = lax.ppermute(back, ("layer", "core"), layer_pairs(-1))
    near = [
        (near.astype(jnp.float32) + part.astype(jnp.float32)).astype(jnp.bfloat16)
        for near, part in zip((near_a, near_b), across)
    ]
    lower_panel, near[1] = lax.optimization_barrier((lower_panel, near[1]))
    (kept,) = multiply(True, place, mask, lower_panel, upper)
    near = [lax.ppermute(part, ("layer", "core"), layer_pairs(1)) for part in near]
    total = kept.astype(jnp.float32) + back.astype(jnp.float32)
    total = ancestor_block.astype(jnp.float32) - total
    columns = near[0].shape[1]
    halves = [
        total[:, k * columns : (k + 1) * columns] - part.astype(jnp.float32)
        for k, part in enumerate(near)
    ]
    return jnp.concatenate(halves, axis=1).astype(jnp.bfloat16)


def solution(mesh):
    fine = Mesh(mesh.devices.reshape(4, 4, 8, 2, 2), AXES)
    col = ("deep", "half", "core")
    placed = (
        P("layer", None, col, "row"),
        P("layer", "row", None),
        P("layer", None, ("row",) + col),
        P("layer", None, None),
        P("layer", None),
        P(("layer",) + col, "row"),
    )
    return jax.shard_map(
        shards, mesh=fine, in_specs=placed, out_specs=P(("layer",) + col, "row"), check_vma=False
    )
```

```python
import functools

import jax
import jax.numpy as jnp
from jax import lax
from jax.experimental import pallas as pl
from jax.experimental.pallas import tpu as pltpu
from jax.sharding import Mesh
from jax.sharding import PartitionSpec as P

AXES = ("layer", "row", "deep", "half", "core")
SWAP = [(0, 1), (1, 0)]
PIECES = 2
SHARES = 4
MULTIPLY_VMEM = 48 << 20


def layer_pairs(step):
    pairs = []
    for x in range(4):
        pairs.append((x * 2, (x + step) % 4 * 2))
        pairs.append((x * 2 + 1, (x - step) % 4 * 2 + 1))
    return pairs


def dot(a, b, contract):
    return lax.dot_general(a, b, (contract, ((), ())), preferred_element_type=jnp.float32)


def spread(x, axis):
    copies = jnp.broadcast_to(x[None], (lax.axis_size(axis),) + x.shape)
    return lax.all_to_all(copies, axis, 0, 0, tiled=True)


def place_kernel(rows, held, part, out, sem):
    count = part.shape[0]
    copy = pltpu.make_async_copy(part, out.at[rows : rows + count, :], sem)
    copy.start()
    copy.wait()


def stage_kernel(part, out):
    count = part.shape[0]
    out[:count, :] = part[...]
    out[count:, :] = jnp.zeros_like(part)


def stage(own):
    rows, width = own.shape
    vmem = pl.BlockSpec(memory_space=pltpu.VMEM)
    return pl.pallas_call(
        stage_kernel,
        out_shape=jax.ShapeDtypeStruct((2 * rows, width), own.dtype),
        in_specs=[vmem],
        out_specs=vmem,
        compiler_params=pltpu.CompilerParams(vmem_limit_bytes=32 << 20),
    )(own)


def put_far(held, far):
    return pl.pallas_call(
        functools.partial(place_kernel, far.shape[0]),
        out_shape=jax.ShapeDtypeStruct(held.shape, held.dtype),
        in_specs=[pl.BlockSpec(memory_space=pl.ANY)] * 2,
        out_specs=pl.BlockSpec(memory_space=pl.ANY),
        scratch_shapes=[pltpu.SemaphoreType.DMA],
        input_output_aliases={0: 0},
        compiler_params=pltpu.CompilerParams(vmem_limit_bytes=32 << 20),
    )(held, far)


def multiply_kernel(first, place, mask, lower, *refs):
    uppers, outs, (rows, panel) = refs[:SHARES], refs[SHARES:-2], refs[-2:]
    strip = lower.shape[1]

    @pl.when(pl.program_id(0) == 0)
    def _():
        for k in range(rows.shape[0] // strip):
            rows[k * strip : (k + 1) * strip, :] = lower[place[first + k]]

    half = place[4]
    share = uppers[0].shape[0] // strip
    for n in range(SHARES * share):
        z, core, k = n // 4, n // 2 % 2, n % 2
        to = (4 * z + core) * strip + jnp.where(half == k, 0, 2 * strip)
        block = uppers[n // share][n % share * strip : (n % share + 1) * strip, :]
        panel[pl.ds(pl.multiple_of(to, 16), strip), :] = block
    value = (dot(rows[...], panel[...], ((1,), (1,))) * mask[...]).astype(jnp.bfloat16)
    if first:
        outs[0][...] = value
        return
    across_a, across_b, near_a, near_b, back = outs

    @pl.when(pl.program_id(0) < PIECES // 2)
    def _():
        across_a[...] = value[:strip, :]
        near_a[...] = value[2 * strip : 3 * strip, :]

    @pl.when(pl.program_id(0) >= PIECES // 2)
    def _():
        across_b[...] = value[:strip, :]
        near_b[...] = value[2 * strip : 3 * strip, :]

    back[...] = value[strip : 2 * strip, :]


def multiply(kept, place, mask, lower, upper):
    groups, strip, width = lower.shape
    columns = upper.shape[0]
    piece = columns // PIECES
    half = PIECES // 2
    out = pl.BlockSpec((strip, piece), lambda i: (0, i))
    first = pl.BlockSpec((strip, piece), lambda i: (0, jnp.minimum(i, half - 1)))
    second = pl.BlockSpec((strip, piece), lambda i: (0, jnp.maximum(i - half, 0)))
    part = jax.ShapeDtypeStruct((strip, columns // 2), jnp.bfloat16)
    whole = jax.ShapeDtypeStruct((strip, columns), jnp.bfloat16)
    shares = [
        pl.BlockSpec((piece // SHARES, width), lambda i, k=k: (i * SHARES + k, 0))
        for k in range(SHARES)
    ]
    return pl.pallas_call(
        functools.partial(multiply_kernel, 3 if kept else 0),
        grid=(PIECES,),
        out_shape=(whole,) if kept else (part,) * 4 + (whole,),
        in_specs=[
            pl.BlockSpec(memory_space=pltpu.SMEM),
            pl.BlockSpec((1, piece), lambda i: (0, i)),
            pl.BlockSpec(lower.shape, lambda i: (0, 0, 0)),
        ] + shares,
        out_specs=(out,) if kept else (first, second, first, second, out),
        scratch_shapes=[
            pltpu.VMEM(((1 if kept else 3) * strip, width), jnp.bfloat16),
            pltpu.VMEM((piece, width), jnp.bfloat16),
        ],
        compiler_params=pltpu.CompilerParams(vmem_limit_bytes=MULTIPLY_VMEM),
    )(place, mask, lower, *([upper] * SHARES))


def shards(
    lower_coupling, upper_inverse, upper_coupling, lower_inverse, row_pattern, ancestor_block
):
    groups, slab_rows = lower_coupling.shape[1:3]
    width = lower_inverse.shape[1]
    layer_index = lax.axis_index("layer")
    row_index = lax.axis_index("row")
    half_index = lax.axis_index("half")
    deep_index = lax.axis_index("deep")
    core_index = lax.axis_index("core")
    slab = ((row_index * 8 + deep_index) * 2 + half_index) * 2 + core_index

    coupling_t = upper_coupling[0].T
    other = lax.ppermute(coupling_t, "half", SWAP)
    solver = dot(upper_inverse[0], lower_inverse[0], ((1,), (0,))).astype(jnp.bfloat16)
    coupling = lower_coupling[0].reshape(groups * slab_rows, -1)
    partial_value = dot(coupling, solver, ((1,), (0,))).astype(jnp.bfloat16)
    held = stage(coupling_t)
    other, partial_value, held = lax.optimization_barrier((other, partial_value, held))
    both = put_far(held, other)
    upper = lax.all_gather(both, ("deep", "core"), axis=0, tiled=True)
    arrived = lax.all_to_all(
        partial_value.reshape(groups, slab_rows, width), "row", 0, 0, tiled=True
    )
    row_mask = lax.dynamic_slice_in_dim(row_pattern[0], slab * slab_rows, slab_rows, 0)
    row_mask = row_mask.reshape(slab_rows, 1).astype(jnp.float32)
    lower_mine = jnp.sum(arrived.astype(jnp.float32), axis=0) * row_mask
    lower_panel = spread(lower_mine.astype(jnp.bfloat16), "row")
    mask = lax.dynamic_slice_in_dim(
        row_pattern[0], row_index * (groups * 8 * slab_rows), groups * 8 * slab_rows, 0
    )
    mask = mask.reshape(1, -1).astype(jnp.float32)

    onward = jnp.where(core_index == 0, 1, 3)
    targets = (layer_index + jnp.stack([2 * onward, 3 * onward, onward, 0 * onward])) % groups
    place = jnp.concatenate([targets, half_index[None]]).astype(jnp.int32)
    across_a, across_b, near_a, near_b, back = multiply(False, place, mask, lower_panel, upper)
    across = [lax.ppermute(part, ("layer", "core"), layer_pairs(1)) for part in (across_a, across_b)]
    back = lax.ppermute(back, ("layer", "core"), layer_pairs(-1))
    near = [
        (near.astype(jnp.float32) + part.astype(jnp.float32)).astype(jnp.bfloat16)
        for near, part in zip((near_a, near_b), across)
    ]
    lower_panel, near[1] = lax.optimization_barrier((lower_panel, near[1]))
    (kept,) = multiply(True, place, mask, lower_panel, upper)
    near = [lax.ppermute(part, ("layer", "core"), layer_pairs(1)) for part in near]
    total = kept.astype(jnp.float32) + back.astype(jnp.float32)
    total = ancestor_block.astype(jnp.float32) - total
    columns = near[0].shape[1]
    halves = [
        total[:, k * columns : (k + 1) * columns] - part.astype(jnp.float32)
        for k, part in enumerate(near)
    ]
    return jnp.concatenate(halves, axis=1).astype(jnp.bfloat16)


def solution(mesh):
    fine = Mesh(mesh.devices.reshape(4, 4, 8, 2, 2), AXES)
    col = ("deep", "half", "core")
    placed = (
        P("layer", None, col, "row"),
        P("layer", "row", None),
        P("layer", None, ("row",) + col),
        P("layer", None, None),
        P("layer", None),
        P(("layer",) + col, "row"),
    )
    return jax.shard_map(
        shards, mesh=fine, in_specs=placed, out_specs=P(("layer",) + col, "row"), check_vma=False
    )
```

```python
import functools

import jax
import jax.numpy as jnp
from jax import lax
from jax.experimental import pallas as pl
from jax.experimental.pallas import tpu as pltpu
from jax.sharding import Mesh
from jax.sharding import PartitionSpec as P

AXES = ("layer", "row", "deep", "half", "core")
SWAP = [(0, 1), (1, 0)]
PIECES = 2
SHARES = 2
MULTIPLY_VMEM = 48 << 20


def layer_pairs(step):
    pairs = []
    for x in range(4):
        pairs.append((x * 2, (x + step) % 4 * 2))
        pairs.append((x * 2 + 1, (x - step) % 4 * 2 + 1))
    return pairs


def dot(a, b, contract):
    return lax.dot_general(a, b, (contract, ((), ())), preferred_element_type=jnp.float32)


def spread(x, axis):
    copies = jnp.broadcast_to(x[None], (lax.axis_size(axis),) + x.shape)
    return lax.all_to_all(copies, axis, 0, 0, tiled=True)


def place_kernel(rows, held, part, out, sem):
    count = part.shape[0]
    copy = pltpu.make_async_copy(part, out.at[rows : rows + count, :], sem)
    copy.start()
    copy.wait()


def stage_kernel(part, out):
    count = part.shape[0]
    out[:count, :] = part[...]
    out[count:, :] = jnp.zeros_like(part)


def stage(own):
    rows, width = own.shape
    vmem = pl.BlockSpec(memory_space=pltpu.VMEM)
    return pl.pallas_call(
        stage_kernel,
        out_shape=jax.ShapeDtypeStruct((2 * rows, width), own.dtype),
        in_specs=[vmem],
        out_specs=vmem,
        compiler_params=pltpu.CompilerParams(vmem_limit_bytes=32 << 20),
    )(own)


def put_far(held, far):
    return pl.pallas_call(
        functools.partial(place_kernel, far.shape[0]),
        out_shape=jax.ShapeDtypeStruct(held.shape, held.dtype),
        in_specs=[pl.BlockSpec(memory_space=pl.ANY)] * 2,
        out_specs=pl.BlockSpec(memory_space=pl.ANY),
        scratch_shapes=[pltpu.SemaphoreType.DMA],
        input_output_aliases={0: 0},
        compiler_params=pltpu.CompilerParams(vmem_limit_bytes=32 << 20),
    )(held, far)


def multiply_kernel(first, place, mask, lower, *refs):
    uppers, outs, (rows, panel) = refs[:SHARES], refs[SHARES:-2], refs[-2:]
    strip = lower.shape[1]

    @pl.when(pl.program_id(0) == 0)
    def _():
        for k in range(rows.shape[0] // strip):
            rows[k * strip : (k + 1) * strip, :] = lower[place[first + k]]

    half = place[4]
    share = uppers[0].shape[0] // strip
    for n in range(SHARES * share):
        z, core, k = n // 4, n // 2 % 2, n % 2
        to = (4 * z + core) * strip + jnp.where(half == k, 0, 2 * strip)
        block = uppers[n // share][n % share * strip : (n % share + 1) * strip, :]
        panel[pl.ds(pl.multiple_of(to, 16), strip), :] = block
    value = (dot(rows[...], panel[...], ((1,), (1,))) * mask[...]).astype(jnp.bfloat16)
    if first:
        outs[0][...] = value
        return
    across_a, across_b, near_a, near_b, back = outs

    @pl.when(pl.program_id(0) < PIECES // 2)
    def _():
        across_a[...] = value[:strip, :]
        near_a[...] = value[2 * strip : 3 * strip, :]

    @pl.when(pl.program_id(0) >= PIECES // 2)
    def _():
        across_b[...] = value[:strip, :]
        near_b[...] = value[2 * strip : 3 * strip, :]

    back[...] = value[strip : 2 * strip, :]


def multiply(kept, place, mask, lower, upper):
    groups, strip, width = lower.shape
    columns = upper.shape[0]
    piece = columns // PIECES
    half = PIECES // 2
    out = pl.BlockSpec((strip, piece), lambda i: (0, i))
    first = pl.BlockSpec((strip, piece), lambda i: (0, jnp.minimum(i, half - 1)))
    second = pl.BlockSpec((strip, piece), lambda i: (0, jnp.maximum(i - half, 0)))
    part = jax.ShapeDtypeStruct((strip, columns // 2), jnp.bfloat16)
    whole = jax.ShapeDtypeStruct((strip, columns), jnp.bfloat16)
    shares = [
        pl.BlockSpec((piece // SHARES, width), lambda i, k=k: (i * SHARES + k, 0))
        for k in range(SHARES)
    ]
    return pl.pallas_call(
        functools.partial(multiply_kernel, 3 if kept else 0),
        grid=(PIECES,),
        out_shape=(whole,) if kept else (part,) * 4 + (whole,),
        in_specs=[
            pl.BlockSpec(memory_space=pltpu.SMEM),
            pl.BlockSpec((1, piece), lambda i: (0, i)),
            pl.BlockSpec(lower.shape, lambda i: (0, 0, 0)),
        ] + shares,
        out_specs=(out,) if kept else (first, second, first, second, out),
        scratch_shapes=[
            pltpu.VMEM(((1 if kept else 3) * strip, width), jnp.bfloat16),
            pltpu.VMEM((piece, width), jnp.bfloat16),
        ],
        compiler_params=pltpu.CompilerParams(vmem_limit_bytes=MULTIPLY_VMEM),
    )(place, mask, lower, *([upper] * SHARES))


def shards(
    lower_coupling, upper_inverse, upper_coupling, lower_inverse, row_pattern, ancestor_block
):
    groups, slab_rows = lower_coupling.shape[1:3]
    width = lower_inverse.shape[1]
    layer_index = lax.axis_index("layer")
    row_index = lax.axis_index("row")
    half_index = lax.axis_index("half")
    deep_index = lax.axis_index("deep")
    core_index = lax.axis_index("core")
    slab = ((row_index * 8 + deep_index) * 2 + half_index) * 2 + core_index

    coupling_t = upper_coupling[0].T
    other = lax.ppermute(coupling_t, "half", SWAP)
    solver = dot(upper_inverse[0], lower_inverse[0], ((1,), (0,))).astype(jnp.bfloat16)
    coupling = lower_coupling[0].reshape(groups * slab_rows, -1)
    partial_value = dot(coupling, solver, ((1,), (0,))).astype(jnp.bfloat16)
    held = stage(coupling_t)
    other, partial_value, held = lax.optimization_barrier((other, partial_value, held))
    both = put_far(held, other)
    upper = lax.all_gather(both, ("deep", "core"), axis=0, tiled=True)
    arrived = lax.all_to_all(
        partial_value.reshape(groups, slab_rows, width), "row", 0, 0, tiled=True
    )
    row_mask = lax.dynamic_slice_in_dim(row_pattern[0], slab * slab_rows, slab_rows, 0)
    row_mask = row_mask.reshape(slab_rows, 1).astype(jnp.float32)
    lower_mine = jnp.sum(arrived.astype(jnp.float32), axis=0) * row_mask
    lower_panel = spread(lower_mine.astype(jnp.bfloat16), "row")
    mask = lax.dynamic_slice_in_dim(
        row_pattern[0], row_index * (groups * 8 * slab_rows), groups * 8 * slab_rows, 0
    )
    mask = mask.reshape(1, -1).astype(jnp.float32)

    onward = jnp.where(core_index == 0, 1, 3)
    targets = (layer_index + jnp.stack([2 * onward, 3 * onward, onward, 0 * onward])) % groups
    place = jnp.concatenate([targets, half_index[None]]).astype(jnp.int32)
    across_a, across_b, near_a, near_b, back = multiply(False, place, mask, lower_panel, upper)
    across = [lax.ppermute(part, ("layer", "core"), layer_pairs(1)) for part in (across_a, across_b)]
    back = lax.ppermute(back, ("layer", "core"), layer_pairs(-1))
    near = [
        (near.astype(jnp.float32) + part.astype(jnp.float32)).astype(jnp.bfloat16)
        for near, part in zip((near_a, near_b), across)
    ]
    lower_panel, near[1] = lax.optimization_barrier((lower_panel, near[1]))
    (kept,) = multiply(True, place, mask, lower_panel, upper)
    near = [lax.ppermute(part, ("layer", "core"), layer_pairs(1)) for part in near]
    total = kept.astype(jnp.float32) + back.astype(jnp.float32)
    total = ancestor_block.astype(jnp.float32) - total
    columns = near[0].shape[1]
    halves = [
        total[:, k * columns : (k + 1) * columns] - part.astype(jnp.float32)
        for k, part in enumerate(near)
    ]
    return jnp.concatenate(halves, axis=1).astype(jnp.bfloat16)


def solution(mesh):
    fine = Mesh(mesh.devices.reshape(4, 4, 8, 2, 2), AXES)
    col = ("deep", "half", "core")
    placed = (
        P("layer", None, col, "row"),
        P("layer", "row", None),
        P("layer", None, ("row",) + col),
        P("layer", None, None),
        P("layer", None),
        P(("layer",) + col, "row"),
    )
    return jax.shard_map(
        shards, mesh=fine, in_specs=placed, out_specs=P(("layer",) + col, "row"), check_vma=False
    )
```

```python
import functools

import jax
import jax.numpy as jnp
from jax import lax
from jax.experimental import pallas as pl
from jax.experimental.pallas import tpu as pltpu
from jax.sharding import Mesh
from jax.sharding import PartitionSpec as P

AXES = ("layer", "row", "deep", "half", "core")
SWAP = [(0, 1), (1, 0)]
PIECES = 2
SHARES = 2
MULTIPLY_VMEM = 48 << 20


def layer_pairs(step):
    pairs = []
    for x in range(4):
        pairs.append((x * 2, (x + step) % 4 * 2))
        pairs.append((x * 2 + 1, (x - step) % 4 * 2 + 1))
    return pairs


def dot(a, b, contract):
    return lax.dot_general(a, b, (contract, ((), ())), preferred_element_type=jnp.float32)


def spread(x, axis):
    copies = jnp.broadcast_to(x[None], (lax.axis_size(axis),) + x.shape)
    return lax.all_to_all(copies, axis, 0, 0, tiled=True)


def place_kernel(rows, held, part, out, sem):
    count = part.shape[0]
    copy = pltpu.make_async_copy(part, out.at[rows : rows + count, :], sem)
    copy.start()
    copy.wait()


def stage_kernel(part, out):
    count = part.shape[0]
    out[:count, :] = part[...]
    out[count:, :] = jnp.zeros_like(part)


def stage(own):
    rows, width = own.shape
    vmem = pl.BlockSpec(memory_space=pltpu.VMEM)
    return pl.pallas_call(
        stage_kernel,
        out_shape=jax.ShapeDtypeStruct((2 * rows, width), own.dtype),
        in_specs=[vmem],
        out_specs=vmem,
        compiler_params=pltpu.CompilerParams(vmem_limit_bytes=32 << 20),
    )(own)


def put_far(held, far):
    return pl.pallas_call(
        functools.partial(place_kernel, far.shape[0]),
        out_shape=jax.ShapeDtypeStruct(held.shape, held.dtype),
        in_specs=[pl.BlockSpec(memory_space=pl.ANY)] * 2,
        out_specs=pl.BlockSpec(memory_space=pl.ANY),
        scratch_shapes=[pltpu.SemaphoreType.DMA],
        input_output_aliases={0: 0},
        compiler_params=pltpu.CompilerParams(vmem_limit_bytes=32 << 20),
    )(held, far)


def multiply_kernel(first, place, mask, lower, *refs):
    uppers, outs, (rows, panel) = refs[:SHARES], refs[SHARES:-2], refs[-2:]
    strip = lower.shape[1]

    @pl.when(pl.program_id(0) == 0)
    def _():
        for k in range(rows.shape[0] // strip):
            rows[k * strip : (k + 1) * strip, :] = lower[place[first + k]]

    half = place[4]
    share = uppers[0].shape[0] // strip
    for n in range(SHARES * share):
        z, core, k = n // 4, n // 2 % 2, n % 2
        to = (4 * z + core) * strip + jnp.where(half == k, 0, 2 * strip)
        block = uppers[n // share][n % share * strip : (n % share + 1) * strip, :]
        panel[pl.ds(pl.multiple_of(to, 16), strip), :] = block
    value = dot(rows[...], panel[...], ((1,), (1,))).astype(jnp.bfloat16) * mask[...]
    if first:
        outs[0][...] = value
        return
    across_a, across_b, near_a, near_b, back = outs

    @pl.when(pl.program_id(0) < PIECES // 2)
    def _():
        across_a[...] = value[:strip, :]
        near_a[...] = value[2 * strip : 3 * strip, :]

    @pl.when(pl.program_id(0) >= PIECES // 2)
    def _():
        across_b[...] = value[:strip, :]
        near_b[...] = value[2 * strip : 3 * strip, :]

    back[...] = value[strip : 2 * strip, :]


def multiply(kept, place, mask, lower, upper):
    groups, strip, width = lower.shape
    columns = upper.shape[0]
    piece = columns // PIECES
    half = PIECES // 2
    out = pl.BlockSpec((strip, piece), lambda i: (0, i))
    first = pl.BlockSpec((strip, piece), lambda i: (0, jnp.minimum(i, half - 1)))
    second = pl.BlockSpec((strip, piece), lambda i: (0, jnp.maximum(i - half, 0)))
    part = jax.ShapeDtypeStruct((strip, columns // 2), jnp.bfloat16)
    whole = jax.ShapeDtypeStruct((strip, columns), jnp.bfloat16)
    shares = [
        pl.BlockSpec((piece // SHARES, width), lambda i, k=k: (i * SHARES + k, 0))
        for k in range(SHARES)
    ]
    return pl.pallas_call(
        functools.partial(multiply_kernel, 3 if kept else 0),
        grid=(PIECES,),
        out_shape=(whole,) if kept else (part,) * 4 + (whole,),
        in_specs=[
            pl.BlockSpec(memory_space=pltpu.SMEM),
            pl.BlockSpec((1, piece), lambda i: (0, i)),
            pl.BlockSpec(lower.shape, lambda i: (0, 0, 0)),
        ] + shares,
        out_specs=(out,) if kept else (first, second, first, second, out),
        scratch_shapes=[
            pltpu.VMEM(((1 if kept else 3) * strip, width), jnp.bfloat16),
            pltpu.VMEM((piece, width), jnp.bfloat16),
        ],
        compiler_params=pltpu.CompilerParams(vmem_limit_bytes=MULTIPLY_VMEM),
    )(place, mask, lower, *([upper] * SHARES))


def shards(
    lower_coupling, upper_inverse, upper_coupling, lower_inverse, row_pattern, ancestor_block
):
    groups, slab_rows = lower_coupling.shape[1:3]
    width = lower_inverse.shape[1]
    layer_index = lax.axis_index("layer")
    row_index = lax.axis_index("row")
    half_index = lax.axis_index("half")
    deep_index = lax.axis_index("deep")
    core_index = lax.axis_index("core")
    slab = ((row_index * 8 + deep_index) * 2 + half_index) * 2 + core_index

    coupling_t = upper_coupling[0].T
    other = lax.ppermute(coupling_t, "half", SWAP)
    solver = dot(upper_inverse[0], lower_inverse[0], ((1,), (0,))).astype(jnp.bfloat16)
    coupling = lower_coupling[0].reshape(groups * slab_rows, -1)
    partial_value = dot(coupling, solver, ((1,), (0,))).astype(jnp.bfloat16)
    held = stage(coupling_t)
    other, partial_value, held = lax.optimization_barrier((other, partial_value, held))
    both = put_far(held, other)
    upper = lax.all_gather(both, ("deep", "core"), axis=0, tiled=True)
    arrived = lax.all_to_all(
        partial_value.reshape(groups, slab_rows, width), "row", 0, 0, tiled=True
    )
    row_mask = lax.dynamic_slice_in_dim(row_pattern[0], slab * slab_rows, slab_rows, 0)
    row_mask = row_mask.reshape(slab_rows, 1).astype(jnp.float32)
    lower_mine = jnp.sum(arrived.astype(jnp.float32), axis=0) * row_mask
    lower_panel = spread(lower_mine.astype(jnp.bfloat16), "row")
    mask = lax.dynamic_slice_in_dim(
        row_pattern[0], row_index * (groups * 8 * slab_rows), groups * 8 * slab_rows, 0
    )
    mask = mask.reshape(1, -1).astype(jnp.bfloat16)

    onward = jnp.where(core_index == 0, 1, 3)
    targets = (layer_index + jnp.stack([2 * onward, 3 * onward, onward, 0 * onward])) % groups
    place = jnp.concatenate([targets, half_index[None]]).astype(jnp.int32)
    across_a, across_b, near_a, near_b, back = multiply(False, place, mask, lower_panel, upper)
    across = [lax.ppermute(part, ("layer", "core"), layer_pairs(1)) for part in (across_a, across_b)]
    back = lax.ppermute(back, ("layer", "core"), layer_pairs(-1))
    near = [
        (near.astype(jnp.float32) + part.astype(jnp.float32)).astype(jnp.bfloat16)
        for near, part in zip((near_a, near_b), across)
    ]
    lower_panel, near[1] = lax.optimization_barrier((lower_panel, near[1]))
    (kept,) = multiply(True, place, mask, lower_panel, upper)
    near = [lax.ppermute(part, ("layer", "core"), layer_pairs(1)) for part in near]
    total = kept.astype(jnp.float32) + back.astype(jnp.float32)
    total = ancestor_block.astype(jnp.float32) - total
    columns = near[0].shape[1]
    halves = [
        total[:, k * columns : (k + 1) * columns] - part.astype(jnp.float32)
        for k, part in enumerate(near)
    ]
    return jnp.concatenate(halves, axis=1).astype(jnp.bfloat16)


def solution(mesh):
    fine = Mesh(mesh.devices.reshape(4, 4, 8, 2, 2), AXES)
    col = ("deep", "half", "core")
    placed = (
        P("layer", None, col, "row"),
        P("layer", "row", None),
        P("layer", None, ("row",) + col),
        P("layer", None, None),
        P("layer", None),
        P(("layer",) + col, "row"),
    )
    return jax.shard_map(
        shards, mesh=fine, in_specs=placed, out_specs=P(("layer",) + col, "row"), check_vma=False
    )
```
